256 devices in a mesh: wide: 64 (over z_hi, y, x, core), wall: 4 (over z_lo).
Axes of the slice: x: 4, y: 4, z: 8 (z_hi: 2, z_lo: 4; z = z_hi * 4 + z_lo), core: 2. Of those that a mesh axis runs over, the one named last changes fastest.
Arguments:
- source: float32 [32, 1024, 1024], P('wall', 'wide'), may hold values from -6 to 6
- spacing: float32 [32], replicated, may hold values from 0.5 to 2
Outputs:
- pressure: float32 [32, 1024, 1024], P('wall', 'wide')
The draws below stay inside these ranges and needn't reach their ends.
All inputs are finite; a program needn't handle non-finite values.
Results may differ from the reference program's by a relative error of at most 0.0003.
Values sent between devices are 32-bit elements; how exact they have to be, the bound alone decides.
A program may use at most 64 MiB of HBM per device.

```python
import math
import jax
import jax.numpy as jnp
from jax import lax

X = 1024
Z = 1024
Y = 32


def draw_source(key, part):
    return jnp.clip(jax.random.normal(key, (Y, Z, X), jnp.float32), -6.0, 6.0)


def setup_inputs(seed: int = 0) -> dict:
    seeds = jax.random.split(jax.random.key(seed), 3)
    return {
        "source": draw_source(jax.random.fold_in(seeds[2], 71), 0),
        "spacing": jnp.clip(jnp.exp(jax.random.uniform(seeds[1], (Y,), jnp.float32, math.log(0.5), math.log(2.0))), 0.5, 2.0),
    }


TWO_PI = 2.0 * math.pi


def reference(source, spacing):
    length_x = source.shape[2]
    length_z = source.shape[1]
    count_of_modes = length_x // 2
    spectrum = jnp.fft.rfft(source, axis=2)[:, :, :count_of_modes]
    spectrum = jnp.fft.fft(spectrum, axis=1)
    stream_modes = jnp.arange(count_of_modes, dtype=jnp.int32).astype(jnp.float32)
    span_int = jnp.arange(length_z, dtype=jnp.int32)
    span_modes = jnp.where(span_int < length_z // 2, span_int, span_int - length_z).astype(jnp.float32)
    stream_wave = stream_modes * (TWO_PI / length_x)
    span_wave = span_modes * (TWO_PI / length_z)
    wave_square = (span_wave * span_wave)[:, None] + (stream_wave * stream_wave)[None, :]
    interior = 2.0 / (spacing[:-1] + spacing[1:])
    lower_all = jnp.concatenate([2.0 / spacing[:1], interior])
    upper_all = jnp.concatenate([interior, 2.0 / spacing[-1:]])

    def forward(carried, row_data):
        pivot_prev, offset_prev = carried
        lower_row, upper_row, spacing_row, source_row = row_data
        divisor = -(lower_row + upper_row) - wave_square * spacing_row - lower_row * pivot_prev
        pivot_now = upper_row / divisor
        offset_now = (spacing_row * source_row - lower_row * offset_prev) / divisor
        return (pivot_now, offset_now), (pivot_now, offset_now)

    start = (jnp.zeros_like(wave_square), jnp.zeros_like(spectrum[0]))
    unused_value, (pivot_rows, offset_rows) = lax.scan(forward, start, (lower_all, upper_all, spacing, spectrum))

    def backward(following, row_data):
        pivot_row, offset_row = row_data
        value = offset_row - pivot_row * following
        return value, value

    unused_value, solution = lax.scan(backward, jnp.zeros_like(spectrum[0]), (pivot_rows, offset_rows), reverse=True)
    physical = jnp.fft.ifft(solution, axis=1)
    physical = jnp.concatenate([physical, jnp.zeros_like(physical[:, :, :1])], axis=2)
    return jnp.fft.irfft(physical, n=length_x, axis=2).astype(jnp.float32)
```

```python
import functools
import math

import jax
import jax.numpy as jnp
import ml_dtypes
import numpy as np
from jax import lax
from jax.experimental import pallas as pl
from jax.experimental.pallas import tpu as pltpu
from jax.sharding import PartitionSpec as P

MESH = pl.DeviceIdType.MESH
TWO_PI = 2.0 * math.pi
X = 1024
Z = 1024
ROWS = 32
WALL = 4
WIDE = 64
SLOTS = WALL * WIDE
ROWS_HERE = ROWS // WALL
SPAN_HERE = Z // WIDE
PIECE = 4


def split_pair(table):
    high = table.astype(ml_dtypes.bfloat16)
    low = (table - high.astype(np.float64)).astype(ml_dtypes.bfloat16)
    return high, low


@functools.cache
def tables():
    x = np.arange(X // 2)
    stream = []
    for parity in range(2):
        mode = 2 * np.arange(128)[:, None] + parity + 256 * np.arange(2)[None, :]
        angle = TWO_PI * ((mode[..., None] * x) % X) / X
        block = np.stack([np.cos(angle), -np.sin(angle)], axis=1)
        stream.append(block.reshape(512, 512))
    stream = np.concatenate(stream, axis=0)

    def complex_block(angle):
        cos, sin = np.cos(angle), np.sin(angle)
        return np.stack([np.stack([cos, sin], 1), np.stack([-sin, cos], 1)], 0)

    outer = np.arange(64)
    block = complex_block(TWO_PI * ((outer[:, None] * outer[None, :]) % 64) / 64)
    span_outer = np.einsum("parq,kl->pkaqrl", block, np.eye(2)).reshape(256, 256)
    inner = np.arange(16)
    block = complex_block(TWO_PI * ((inner[:, None] * inner[None, :]) % 16) / 16)
    span_inner = np.einsum("pbrl,yz->ypbrzl", block, np.eye(ROWS_HERE)).reshape(256, 256)
    angle = TWO_PI * (outer[:, None] * inner[None, :]) / Z
    angle = np.broadcast_to(angle[None, :, None, :], (2, 64, ROWS_HERE, 16)).reshape(128, 128)
    twist = np.stack([np.cos(angle), np.sin(angle), np.cos(angle).T, np.sin(angle).T])
    small = np.concatenate([span_outer, span_inner, span_inner.T, span_outer.T], axis=0)
    return split_pair(stream) + split_pair(small) + (twist.astype(np.float32),)


def deltas():
    steps = [
        (y, x, core, z)
        for y in range(4)
        for x in range(4)
        for core in range(2)
        for z in range(8)
        if (y, x, core, z) != (0, 0, 0, 0)
    ]
    hops = lambda d: min(d[0], 4 - d[0]) + min(d[1], 4 - d[1]) + min(d[3], 8 - d[3])
    return sorted(steps, key=lambda d: -hops(d))


def dot3(high, low, value, contract):
    dims = (contract, ((), ()))
    value_high = value.astype(jnp.bfloat16)
    value_low = (value - value_high.astype(jnp.float32)).astype(jnp.bfloat16)
    dot = functools.partial(lax.dot_general, dimension_numbers=dims, preferred_element_type=jnp.float32)
    return dot(high, value_high) + (dot(high, value_low) + dot(low, value_high))


NN = ((1,), (0,))
NT = ((1,), (1,))


def kernel(
    spacing, source, stream_high, stream_low, small_high, small_low, twist, out,
    send_a, recv_a, send_b, recv_b, gain, carry, pivot, work, solved,
    send_sem, recv_sem, own_sem,
):
    wide, wall = lax.axis_index("wide"), lax.axis_index("wall")
    slot = wall * WIDE + wide
    core = lax.rem(wide, 2)
    x = lax.rem(lax.div(wide, 2), 4)
    y = lax.rem(lax.div(wide, 8), 4)
    z = lax.div(wide, 32) * 4 + wall
    at_core = [lax.rem(core + d, 2) for d in range(2)]
    at_x = [lax.rem(x + d, 4) * 2 for d in range(4)]
    at_y = [lax.rem(y + d, 4) * 8 for d in range(4)]
    z_all = [lax.rem(z + d, 8) for d in range(8)]
    at_high = [lax.div(v, 4) * 32 for v in z_all]
    at_wall = [lax.rem(v, 4) for v in z_all]

    def target(d):
        return at_y[d[0]] + at_x[d[1]] + at_core[d[2]] + at_high[d[3]], at_wall[d[3]]

    order = deltas()
    barrier = pltpu.get_barrier_semaphore()
    for d in order:
        to_wide, to_wall = target(d)
        pl.semaphore_signal(
            barrier, inc=1, device_id={"wide": to_wide, "wall": to_wall}, device_id_type=MESH
        )

    def exchange(index, send, recv):
        mine = pl.ds(pl.multiple_of(slot * PIECE, PIECE), PIECE)
        own = pltpu.make_async_copy(send.at[mine], recv.at[mine], own_sem.at[index])
        own.start()
        for d in order:
            to_wide, to_wall = target(d)
            there = pl.multiple_of((to_wall * WIDE + to_wide) * PIECE, PIECE)
            pltpu.make_async_remote_copy(
                src_ref=send.at[pl.ds(there, PIECE)],
                dst_ref=recv.at[mine],
                send_sem=send_sem.at[index],
                recv_sem=recv_sem.at[index],
                device_id={"wide": to_wide, "wall": to_wall},
                device_id_type=MESH,
            ).start()
        own.wait()
        rest = pl.ds(0, (SLOTS - 1) * PIECE)
        pltpu.make_async_copy(send.at[rest], recv.at[rest], recv_sem.at[index]).wait()

    def sent(index, send, recv):
        rest = pl.ds(0, (SLOTS - 1) * PIECE)
        pltpu.make_async_copy(send.at[rest], recv.at[rest], send_sem.at[index]).wait()

    left, right = source[:, : X // 2], source[:, X // 2 :]
    for parity, half in enumerate((left + right, left - right)):
        rows = pl.ds(512 * parity, 512)
        send_a[rows, :] = dot3(stream_high[rows, :], stream_low[rows, :], half, NT)

    lanes = lax.broadcasted_iota(jnp.int32, (16, 128), 1)
    digit = lax.broadcasted_iota(jnp.int32, (16, 128), 0)
    upper_half = lanes >= 64
    kx = 2 * lax.rem(slot, 128) + lax.div(slot, 128) + jnp.where(upper_half, 256, 0)
    kz = 64 * digit + jnp.where(upper_half, lanes - 64, lanes)
    kz = jnp.where(kz < Z // 2, kz, kz - Z)
    stream_wave = kx.astype(jnp.float32) * (TWO_PI / X)
    span_wave = kz.astype(jnp.float32) * (TWO_PI / Z)
    wave_square = span_wave * span_wave + stream_wave * stream_wave
    widths = [jnp.full((16, 128), spacing[j], jnp.float32) for j in range(ROWS)]
    edges = (
        [2.0 / widths[0]]
        + [2.0 / (widths[j] + widths[j + 1]) for j in range(ROWS - 1)]
        + [2.0 / widths[ROWS - 1]]
    )
    previous = jnp.zeros((16, 128), jnp.float32)
    for j in range(ROWS):
        lower, upper = edges[j], edges[j + 1]
        inverse = 1.0 / (-(lower + upper) - wave_square * widths[j] - lower * previous)
        previous = upper * inverse
        pivot[j] = previous
        gain[j] = widths[j] * inverse
        carry[j] = lower * inverse
    weight = jnp.where(kx[:1] == 0, 1.0, 2.0) * (1.0 / (X * Z))

    pl.semaphore_wait(barrier, SLOTS - 1)
    exchange(0, send_a, recv_a)

    offset_re = jnp.zeros((16, 128), jnp.float32)
    offset_im = jnp.zeros((16, 128), jnp.float32)
    for block in range(WALL):
        rows = pl.ds(256 * block, 256)
        mixed = dot3(small_high[0:256, :], small_low[0:256, :], recv_a[rows, :], NN)
        re, im = mixed[:128], mixed[128:]
        cos, sin = twist[0], twist[1]
        turned = jnp.concatenate([re * cos + im * sin, im * cos - re * sin], axis=1)
        work[...] = dot3(small_high[256:512, :], small_low[256:512, :], turned, NT)
        for j in range(ROWS_HERE):
            row = block * ROWS_HERE + j
            offset_re = gain[row] * work[pl.ds(32 * j, 16), :] - carry[row] * offset_re
            offset_im = gain[row] * work[pl.ds(32 * j + 16, 16), :] - carry[row] * offset_im
            solved[pl.ds(32 * row, 16), :] = offset_re
            solved[pl.ds(32 * row + 16, 16), :] = offset_im
    value_re = offset_re
    value_im = offset_im
    for row in range(ROWS - 2, -1, -1):
        value_re = solved[pl.ds(32 * row, 16), :] - pivot[row] * value_re
        value_im = solved[pl.ds(32 * row + 16, 16), :] - pivot[row] * value_im
        solved[pl.ds(32 * row, 16), :] = value_re
        solved[pl.ds(32 * row + 16, 16), :] = value_im

    cos, sin = twist[2] * weight, twist[3] * weight
    for block in range(WALL):
        rows = pl.ds(256 * block, 256)
        mixed = dot3(small_high[512:768, :], small_low[512:768, :], solved[rows, :], NN)
        re, im = mixed[:128], mixed[128:]
        turned = jnp.concatenate([re * cos - im * sin, im * cos + re * sin], axis=1)
        send_b[rows, :] = dot3(small_high[768:1024, :], small_low[768:1024, :], turned, NT)

    exchange(1, send_b, recv_b)

    halves = []
    for parity in range(2):
        rows = pl.ds(512 * parity, 512)
        value = recv_b[rows, :].T
        value_high = value.astype(jnp.bfloat16)
        value_low = (value - value_high.astype(jnp.float32)).astype(jnp.bfloat16)
        dot = functools.partial(jnp.dot, preferred_element_type=jnp.float32)
        halves.append(
            dot(value_high, stream_high[rows, :])
            + (dot(value_low, stream_high[rows, :]) + dot(value_high, stream_low[rows, :]))
        )
    out[:, : X // 2] = halves[0] + halves[1]
    out[:, X // 2 :] = halves[0] - halves[1]
    sent(0, send_a, recv_a)
    sent(1, send_b, recv_b)


def shards(source, spacing):
    vmem = pl.BlockSpec(memory_space=pltpu.VMEM)
    plane = pltpu.VMEM((1024, 128), jnp.float32)
    coefficient = pltpu.VMEM((ROWS, 16, 128), jnp.float32)
    pressure = pl.pallas_call(
        kernel,
        out_shape=jax.ShapeDtypeStruct((ROWS_HERE * SPAN_HERE, X), jnp.float32),
        in_specs=[pl.BlockSpec(memory_space=pltpu.SMEM)] + [vmem] * 6,
        out_specs=vmem,
        scratch_shapes=[
            plane, plane, plane, plane, coefficient, coefficient, coefficient,
            pltpu.VMEM((256, 128), jnp.float32), plane,
            pltpu.SemaphoreType.DMA((2,)),
            pltpu.SemaphoreType.DMA((2,)),
            pltpu.SemaphoreType.DMA((2,)),
        ],
        compiler_params=pltpu.CompilerParams(
            collective_id=0, has_side_effects=True, vmem_limit_bytes=48 * 1024 * 1024
        ),
    )(spacing, source.reshape(ROWS_HERE * SPAN_HERE, X), *(jnp.asarray(t) for t in tables()))
    return pressure.reshape(source.shape)


def solution(mesh):
    in_specs = (P("wall", "wide", None), P())
    out_specs = P("wall", "wide", None)
    return jax.shard_map(shards, mesh=mesh, in_specs=in_specs, out_specs=out_specs, check_vma=False)
```

```python
import functools
import math

import jax
import jax.numpy as jnp
import ml_dtypes
import numpy as np
from jax import lax
from jax.experimental import pallas as pl
from jax.experimental.pallas import tpu as pltpu
from jax.sharding import PartitionSpec as P

MESH = pl.DeviceIdType.MESH
TWO_PI = 2.0 * math.pi
X = 1024
Z = 1024
ROWS = 32
WALL = 4
WIDE = 64
SLOTS = WALL * WIDE
ROWS_HERE = ROWS // WALL
SPAN_HERE = Z // WIDE
PIECE = 2


def split_pair(table):
    high = table.astype(ml_dtypes.bfloat16)
    low = (table - high.astype(np.float64)).astype(ml_dtypes.bfloat16)
    return high, low


@functools.cache
def tables():
    x = np.arange(X // 2)
    slot = np.arange(SLOTS)
    mode = (2 * (slot % 128) + slot // 128)[None, :] + 256 * np.arange(2)[:, None]
    angle = TWO_PI * ((mode[..., None] * x) % X) / X
    stream = np.stack([np.cos(angle), -np.sin(angle)], axis=2).reshape(1024, 512)

    outer, inner = np.arange(64), np.arange(SPAN_HERE)
    angle = TWO_PI * ((outer[:, None] * outer[None, :]) % 64) / 64
    cos, sin = np.cos(angle), np.sin(angle)
    first = np.stack([np.stack([cos, sin], 2), np.stack([-sin, cos], 2)], 0)
    first = first.reshape(128, 128)
    angle = TWO_PI * ((inner[:, None] * inner[None, :]) % SPAN_HERE) / SPAN_HERE
    every_row = np.eye(ROWS_HERE)
    cos, sin = np.kron(every_row, np.cos(angle)), np.kron(every_row, np.sin(angle))
    angle = np.tile(TWO_PI * (outer[:, None] * inner[None, :]) / Z, (1, ROWS_HERE))
    turn_cos, turn_sin = np.cos(angle), np.sin(angle)
    twist = np.concatenate([turn_cos, turn_sin], axis=0)
    back_cos = np.concatenate([turn_cos.T, turn_cos.T], axis=1)
    back_sin = np.concatenate([-turn_sin.T, turn_sin.T], axis=1)
    small = np.concatenate(
        [first, first.T, cos, sin, twist, back_cos, back_sin], axis=1
    )
    small = np.pad(small, ((0, 0), (0, 128))).reshape(128, 2, 512).transpose(1, 0, 2).reshape(256, 512)
    return np.concatenate(split_pair(stream) + split_pair(small), axis=0)


def deltas():
    steps = [
        (y, x, core, z)
        for y in range(4)
        for x in range(4)
        for core in range(2)
        for z in range(8)
        if (y, x, core, z) != (0, 0, 0, 0)
    ]
    hops = lambda d: min(d[0], 4 - d[0]) + min(d[1], 4 - d[1])
    return sorted(steps, key=lambda d: (-hops(d), -min(d[3], 8 - d[3])))


def halves_of(value):
    high = value.astype(jnp.bfloat16)
    return high, (value - high.astype(jnp.float32)).astype(jnp.bfloat16)


def dot3(left, right, contract):
    dot = functools.partial(
        lax.dot_general,
        dimension_numbers=(contract, ((), ())),
        preferred_element_type=jnp.float32,
    )
    return dot(left[0], right[0]) + (dot(left[0], right[1]) + dot(left[1], right[0]))


NN = ((1,), (0,))
NT = ((1,), (1,))


def kernel(
    spacing_far, source_far, packed_far, out,
    spacing, source, packed,
    send_a, recv_a, send_b, recv_b, gain, carry, pivot, solved,
    send_sem, recv_sem, own_sem, load_sem,
):
    wide, wall = lax.axis_index("wide"), lax.axis_index("wall")
    slot = wall * WIDE + wide
    core = lax.rem(wide, 2)
    x = lax.rem(lax.div(wide, 2), 4)
    y = lax.rem(lax.div(wide, 8), 4)
    z = lax.div(wide, 32) * 4 + wall
    at_core = [lax.rem(core + d, 2) for d in range(2)]
    at_x = [lax.rem(x + d, 4) * 2 for d in range(4)]
    at_y = [lax.rem(y + d, 4) * 8 for d in range(4)]
    z_all = [lax.rem(z + d, 8) for d in range(8)]
    at_high = [lax.div(v, 4) * 32 for v in z_all]
    at_wall = [lax.rem(v, 4) for v in z_all]

    def target(d):
        return at_y[d[0]] + at_x[d[1]] + at_core[d[2]] + at_high[d[3]], at_wall[d[3]]

    order = deltas()
    barrier = pltpu.get_barrier_semaphore()
    for d in order:
        to_wide, to_wall = target(d)
        pl.semaphore_signal(
            barrier, inc=1, device_id={"wide": to_wide, "wall": to_wall}, device_id_type=MESH
        )
    loads = [
        pltpu.make_async_copy(there, here, load_sem.at[index])
        for index, (there, here) in enumerate(
            [
                (source_far, source),
                (packed_far.at[pl.ds(0, 2048)], packed.at[pl.ds(0, 2048)]),
                (spacing_far, spacing),
                (packed_far.at[pl.ds(2048, 512)], packed.at[pl.ds(2048, 512)]),
            ]
        )
    ]
    for load in loads:
        load.start()

    def start(index, k, send, recv):
        index = 2 * index + k
        mine = pl.ds(pl.multiple_of(k * 512 + slot * PIECE, PIECE), PIECE)
        pltpu.make_async_copy(send.at[mine], recv.at[mine], own_sem.at[index]).start()
        for d in order:
            to_wide, to_wall = target(d)
            there = pl.multiple_of(k * 512 + (to_wall * WIDE + to_wide) * PIECE, PIECE)
            pltpu.make_async_remote_copy(
                src_ref=send.at[pl.ds(there, PIECE)],
                dst_ref=recv.at[mine],
                send_sem=send_sem.at[index],
                recv_sem=recv_sem.at[index],
                device_id={"wide": to_wide, "wall": to_wall},
                device_id_type=MESH,
            ).start()

    def arrive(index, k, send, recv):
        index = 2 * index + k
        mine = pl.ds(pl.multiple_of(k * 512 + slot * PIECE, PIECE), PIECE)
        pltpu.make_async_copy(send.at[mine], recv.at[mine], own_sem.at[index]).wait()
        rest = pl.ds(k * 512, (SLOTS - 1) * PIECE)
        pltpu.make_async_copy(send.at[rest], recv.at[rest], recv_sem.at[index]).wait()

    def sent(index, k, send, recv):
        rest = pl.ds(k * 512, (SLOTS - 1) * PIECE)
        pltpu.make_async_copy(send.at[rest], recv.at[rest], send_sem.at[2 * index + k]).wait()

    loads[0].wait()
    loads[1].wait()
    left, right = source[:, : X // 2], source[:, X // 2 :]
    parts = halves_of(left + right), halves_of(left - right)

    def stream_rows(k, parity):
        base = 512 * k + 256 * parity
        return packed[pl.ds(base, 256), :], packed[pl.ds(1024 + base, 256), :]

    for k in range(2):
        for parity in range(2):
            rows = pl.ds(512 * k + 256 * parity, 256)
            send_a[rows, :] = dot3(stream_rows(k, parity), parts[parity], NT)

    loads[2].wait()
    lanes = lax.broadcasted_iota(jnp.int32, (16, 128), 1)
    digit = lax.broadcasted_iota(jnp.int32, (16, 128), 0)
    kz = 64 * digit + jnp.where(lanes >= 64, lanes - 64, lanes)
    kz = jnp.where(kz < Z // 2, kz, kz - Z)
    span_wave = kz.astype(jnp.float32) * (TWO_PI / Z)
    widths = [jnp.full((16, 128), spacing[j], jnp.float32) for j in range(ROWS)]
    edges = (
        [2.0 / widths[0]]
        + [2.0 / (widths[j] + widths[j + 1]) for j in range(ROWS - 1)]
        + [2.0 / widths[ROWS - 1]]
    )
    first_mode = 2 * lax.rem(slot, 128) + lax.div(slot, 128)
    wave_square, previous = [], []
    for k in range(2):
        kx = jnp.full((16, 128), first_mode + 256 * k, jnp.int32)
        stream_wave = kx.astype(jnp.float32) * (TWO_PI / X)
        wave_square.append(span_wave * span_wave + stream_wave * stream_wave)
        previous.append(jnp.zeros((16, 128), jnp.float32))
    for j in range(ROWS):
        lower, upper = edges[j], edges[j + 1]
        for k in range(2):
            divisor = -(lower + upper) - wave_square[k] * widths[j] - lower * previous[k]
            inverse = 1.0 / divisor
            previous[k] = upper * inverse
            pivot[k, j] = previous[k]
            gain[k, j] = widths[j] * inverse
            carry[k, j] = lower * inverse

    loads[3].wait()

    def table(index):
        high, columns = 2048 + 128 * (index // 4), pl.ds(128 * (index % 4), 128)
        return packed[pl.ds(high, 128), columns], packed[pl.ds(high + 256, 128), columns]

    def number(index):
        high, low = table(index)
        return high.astype(jnp.float32) + low.astype(jnp.float32)

    pl.semaphore_wait(barrier, SLOTS - 1)
    start(0, 0, send_a, recv_a)
    start(0, 1, send_a, recv_a)

    for k in range(2):
        arrive(0, k, send_a, recv_a)
        twist = number(4)
        cos, sin = twist[:64], twist[64:]
        wave_cos, wave_sin = table(2), table(3)
        second = tuple(jnp.concatenate([c, s], axis=1) for c, s in zip(wave_cos, wave_sin))
        offset = jnp.zeros((16, 128), jnp.float32)
        for block in range(WALL):
            rows = pl.ds(512 * k + 128 * block, 128)
            mixed = dot3(table(0), halves_of(recv_a[rows, :]), NN)
            re, im = mixed[:64], mixed[64:]
            turned_re = halves_of(re * cos + im * sin)
            turned_im = halves_of(im * cos - re * sin)
            turned = tuple(
                jnp.concatenate(
                    [jnp.concatenate([r, i], axis=1), jnp.concatenate([i, -r], axis=1)], axis=0
                )
                for r, i in zip(turned_re, turned_im)
            )
            work = dot3(second, turned, NT)
            for j in range(ROWS_HERE):
                row = block * ROWS_HERE + j
                offset = gain[k, row] * work[16 * j : 16 * j + 16] - carry[k, row] * offset
                solved[pl.ds(16 * row, 16), :] = offset
        value = offset
        for row in range(ROWS - 2, -1, -1):
            value = solved[pl.ds(16 * row, 16), :] - pivot[k, row] * value
            solved[pl.ds(16 * row, 16), :] = value

        weight = 1.0 / (X * Z)
        kx = jnp.full((1, 128), first_mode + 256 * k, jnp.int32)
        weight = jnp.where(kx == 0, weight, 2.0 * weight)
        cos, sin = number(5) * weight, number(6) * weight
        sign = jnp.where(lanes[:1] < 64, -1.0, 1.0)
        for block in range(WALL):
            rows = pl.ds(512 * k + 128 * block, 128)
            value = halves_of(solved[pl.ds(128 * block, 128), :])
            mixed = dot3(wave_cos, value, NN) + sign * pltpu.roll(dot3(wave_sin, value, NN), 64, 1)
            turned = halves_of(mixed * cos + pltpu.roll(mixed, 64, 1) * sin)
            send_b[rows, :] = dot3(table(1), turned, NT)
        start(1, k, send_b, recv_b)

    sums = [0.0, 0.0]
    for k in range(2):
        arrive(1, k, send_b, recv_b)
        for parity in range(2):
            rows = pl.ds(512 * k + 256 * parity, 256)
            sums[parity] += dot3(halves_of(recv_b[rows, :].T), stream_rows(k, parity), NN)
    out[:, : X // 2] = sums[0] + sums[1]
    out[:, X // 2 :] = sums[0] - sums[1]
    for k in range(2):
        sent(0, k, send_a, recv_a)
        sent(1, k, send_b, recv_b)


def shards(source, spacing):
    plane = pltpu.VMEM((1024, 128), jnp.float32)
    coefficient = pltpu.VMEM((2, ROWS, 16, 128), jnp.float32)
    semaphores = pltpu.SemaphoreType.DMA((4,))
    pressure = pl.pallas_call(
        kernel,
        out_shape=jax.ShapeDtypeStruct((ROWS_HERE * SPAN_HERE, X), jnp.float32),
        in_specs=[pl.BlockSpec(memory_space=pl.ANY)] * 3,
        out_specs=pl.BlockSpec(memory_space=pltpu.VMEM),
        scratch_shapes=[
            pltpu.SMEM((ROWS,), jnp.float32),
            pltpu.VMEM((ROWS_HERE * SPAN_HERE, X), jnp.float32),
            pltpu.VMEM((2560, 512), jnp.bfloat16),
            plane, plane, plane, plane, coefficient, coefficient, coefficient,
            pltpu.VMEM((512, 128), jnp.float32),
            semaphores, semaphores, semaphores, semaphores,
        ],
        compiler_params=pltpu.CompilerParams(
            collective_id=0, has_side_effects=True, vmem_limit_bytes=53 * 1024 * 1024
        ),
    )(spacing, source.reshape(ROWS_HERE * SPAN_HERE, X), jnp.asarray(tables()))
    return pressure.reshape(source.shape)


def solution(mesh):
    in_specs = (P("wall", "wide", None), P())
    out_specs = P("wall", "wide", None)
    return jax.shard_map(shards, mesh=mesh, in_specs=in_specs, out_specs=out_specs, check_vma=False)
```

```python
import functools
import math

import jax
import jax.numpy as jnp
import ml_dtypes
import numpy as np
from jax import lax
from jax.experimental import pallas as pl
from jax.experimental.pallas import tpu as pltpu
from jax.sharding import PartitionSpec as P

MESH = pl.DeviceIdType.MESH
TWO_PI = 2.0 * math.pi
X = 1024
Z = 1024
ROWS = 32
WALL = 4
WIDE = 64
SLOTS = WALL * WIDE
ROWS_HERE = ROWS // WALL
SPAN_HERE = Z // WIDE
PIECE = 2


def split_pair(table):
    high = table.astype(ml_dtypes.bfloat16)
    low = (table - high.astype(np.float64)).astype(ml_dtypes.bfloat16)
    return high, low


@functools.cache
def tables():
    x = np.arange(X // 2)
    slot = np.arange(SLOTS)
    mode = (2 * (slot % 128) + slot // 128)[None, :] + 256 * np.arange(2)[:, None]
    angle = TWO_PI * ((mode[..., None] * x) % X) / X
    stream = np.stack([np.cos(angle), -np.sin(angle)], axis=2).reshape(1024, 512)

    outer, inner = np.arange(64), np.arange(SPAN_HERE)
    angle = TWO_PI * ((outer[:, None] * outer[None, :]) % 64) / 64
    cos, sin = np.cos(angle), np.sin(angle)
    first = np.stack([np.stack([cos, sin], 2), np.stack([-sin, cos], 2)], 0)
    first = first.reshape(128, 128)
    angle = TWO_PI * ((inner[:, None] * inner[None, :]) % SPAN_HERE) / SPAN_HERE
    every_row = np.eye(ROWS_HERE)
    cos, sin = np.kron(every_row, np.cos(angle)), np.kron(every_row, np.sin(angle))
    angle = np.tile(TWO_PI * (outer[:, None] * inner[None, :]) / Z, (1, ROWS_HERE))
    turn_cos, turn_sin = np.cos(angle), np.sin(angle)
    twist = np.concatenate([turn_cos, turn_sin], axis=0)
    back_cos = np.concatenate([turn_cos.T, turn_cos.T], axis=1)
    back_sin = np.concatenate([-turn_sin.T, turn_sin.T], axis=1)
    small = np.concatenate(
        [first, first.T, cos, sin, twist, back_cos, back_sin], axis=1
    )
    small = np.pad(small, ((0, 0), (0, 128))).reshape(128, 2, 512).transpose(1, 0, 2).reshape(256, 512)
    return np.concatenate(split_pair(stream) + split_pair(small), axis=0)


def deltas(spanwise_first):
    steps = [
        (y, x, core, z)
        for y in range(4)
        for x in range(4)
        for core in range(2)
        for z in range(8)
        if (y, x, core, z) != (0, 0, 0, 0)
    ]
    across = lambda d: min(d[0], 4 - d[0]) + min(d[1], 4 - d[1])
    along = lambda d: min(d[3], 8 - d[3])
    if spanwise_first:
        return sorted(steps, key=lambda d: -along(d) - across(d))
    return sorted(steps, key=lambda d: (-across(d), -along(d)))


def halves_of(value):
    high = value.astype(jnp.bfloat16)
    return high, (value - high.astype(jnp.float32)).astype(jnp.bfloat16)


def dot3(left, right, contract):
    dot = functools.partial(
        lax.dot_general,
        dimension_numbers=(contract, ((), ())),
        preferred_element_type=jnp.float32,
    )
    return dot(left[0], right[0]) + (dot(left[0], right[1]) + dot(left[1], right[0]))


NN = ((1,), (0,))
NT = ((1,), (1,))


def kernel(
    spacing_far, source_far, packed_far, out,
    spacing, source, packed,
    send_a, recv_a, send_b, recv_b, gain, carry, pivot, solved,
    send_sem, recv_sem, own_sem, load_sem,
):
    wide, wall = lax.axis_index("wide"), lax.axis_index("wall")
    slot = wall * WIDE + wide
    core = lax.rem(wide, 2)
    x = lax.rem(lax.div(wide, 2), 4)
    y = lax.rem(lax.div(wide, 8), 4)
    z = lax.div(wide, 32) * 4 + wall
    at_core = [lax.rem(core + d, 2) for d in range(2)]
    at_x = [lax.rem(x + d, 4) * 2 for d in range(4)]
    at_y = [lax.rem(y + d, 4) * 8 for d in range(4)]
    z_all = [lax.rem(z + d, 8) for d in range(8)]
    at_high = [lax.div(v, 4) * 32 for v in z_all]
    at_wall = [lax.rem(v, 4) for v in z_all]

    def target(d):
        return at_y[d[0]] + at_x[d[1]] + at_core[d[2]] + at_high[d[3]], at_wall[d[3]]

    loads = [
        pltpu.make_async_copy(there, here, load_sem.at[index])
        for index, (there, here) in enumerate(
            [
                (source_far, source),
                (packed_far.at[pl.ds(0, 512)], packed.at[pl.ds(0, 512)]),
                (packed_far.at[pl.ds(1024, 512)], packed.at[pl.ds(1024, 512)]),
                (packed_far.at[pl.ds(512, 512)], packed.at[pl.ds(512, 512)]),
                (packed_far.at[pl.ds(1536, 512)], packed.at[pl.ds(1536, 512)]),
                (packed_far.at[pl.ds(2048, 512)], packed.at[pl.ds(2048, 512)]),
                (spacing_far, spacing),
            ]
        )
    ]
    for load in loads:
        load.start()
    barrier = pltpu.get_barrier_semaphore()
    for d in deltas(True):
        to_wide, to_wall = target(d)
        pl.semaphore_signal(
            barrier, inc=1, device_id={"wide": to_wide, "wall": to_wall}, device_id_type=MESH
        )
    order = deltas(False)

    def start(index, k, send, recv):
        index = 2 * index + k
        mine = pl.ds(pl.multiple_of(k * 512 + slot * PIECE, PIECE), PIECE)
        pltpu.make_async_copy(send.at[mine], recv.at[mine], own_sem.at[index]).start()
        for d in order:
            to_wide, to_wall = target(d)
            there = pl.multiple_of(k * 512 + (to_wall * WIDE + to_wide) * PIECE, PIECE)
            pltpu.make_async_remote_copy(
                src_ref=send.at[pl.ds(there, PIECE)],
                dst_ref=recv.at[mine],
                send_sem=send_sem.at[index],
                recv_sem=recv_sem.at[index],
                device_id={"wide": to_wide, "wall": to_wall},
                device_id_type=MESH,
            ).start()

    def arrive(index, k, send, recv):
        index = 2 * index + k
        mine = pl.ds(pl.multiple_of(k * 512 + slot * PIECE, PIECE), PIECE)
        pltpu.make_async_copy(send.at[mine], recv.at[mine], own_sem.at[index]).wait()
        rest = pl.ds(k * 512, (SLOTS - 1) * PIECE)
        pltpu.make_async_copy(send.at[rest], recv.at[rest], recv_sem.at[index]).wait()

    def sent(index, k, send, recv):
        rest = pl.ds(k * 512, (SLOTS - 1) * PIECE)
        pltpu.make_async_copy(send.at[rest], recv.at[rest], send_sem.at[2 * index + k]).wait()

    for load in loads[:3]:
        load.wait()
    left, right = source[:, : X // 2], source[:, X // 2 :]
    parts = halves_of(left + right), halves_of(left - right)

    def stream_rows(k, parity):
        base = 512 * k + 256 * parity
        return packed[pl.ds(base, 256), :], packed[pl.ds(1024 + base, 256), :]

    def transform(k):
        for parity in range(2):
            rows = pl.ds(512 * k + 256 * parity, 256)
            send_a[rows, :] = dot3(stream_rows(k, parity), parts[parity], NT)

    transform(0)
    pl.semaphore_wait(barrier, SLOTS - 1)
    start(0, 0, send_a, recv_a)
    for load in loads[3:]:
        load.wait()
    transform(1)
    start(0, 1, send_a, recv_a)

    lanes = lax.broadcasted_iota(jnp.int32, (16, 128), 1)
    digit = lax.broadcasted_iota(jnp.int32, (16, 128), 0)
    kz = 64 * digit + jnp.where(lanes >= 64, lanes - 64, lanes)
    kz = jnp.where(kz < Z // 2, kz, kz - Z)
    span_wave = kz.astype(jnp.float32) * (TWO_PI / Z)
    widths = [jnp.full((16, 128), spacing[j], jnp.float32) for j in range(ROWS)]
    edges = (
        [2.0 / widths[0]]
        + [2.0 / (widths[j] + widths[j + 1]) for j in range(ROWS - 1)]
        + [2.0 / widths[ROWS - 1]]
    )
    first_mode = 2 * lax.rem(slot, 128) + lax.div(slot, 128)
    wave_square, previous = [], []
    for k in range(2):
        kx = jnp.full((16, 128), first_mode + 256 * k, jnp.int32)
        stream_wave = kx.astype(jnp.float32) * (TWO_PI / X)
        wave_square.append(span_wave * span_wave + stream_wave * stream_wave)
        previous.append(jnp.zeros((16, 128), jnp.float32))
    for j in range(ROWS):
        lower, upper = edges[j], edges[j + 1]
        for k in range(2):
            divisor = -(lower + upper) - wave_square[k] * widths[j] - lower * previous[k]
            inverse = 1.0 / divisor
            previous[k] = upper * inverse
            pivot[k, j] = previous[k]
            gain[k, j] = widths[j] * inverse
            carry[k, j] = lower * inverse

    def table(index):
        high, columns = 2048 + 128 * (index // 4), pl.ds(128 * (index % 4), 128)
        return packed[pl.ds(high, 128), columns], packed[pl.ds(high + 256, 128), columns]

    def number(index):
        high, low = table(index)
        return high.astype(jnp.float32) + low.astype(jnp.float32)

    for k in range(2):
        arrive(0, k, send_a, recv_a)
        twist = number(4)
        cos, sin = twist[:64], twist[64:]
        wave_cos, wave_sin = table(2), table(3)
        second = tuple(jnp.concatenate([c, s], axis=1) for c, s in zip(wave_cos, wave_sin))
        offset = jnp.zeros((16, 128), jnp.float32)
        for block in range(WALL):
            rows = pl.ds(512 * k + 128 * block, 128)
            mixed = dot3(table(0), halves_of(recv_a[rows, :]), NN)
            re, im = mixed[:64], mixed[64:]
            turned_re = halves_of(re * cos + im * sin)
            turned_im = halves_of(im * cos - re * sin)
            turned = tuple(
                jnp.concatenate(
                    [jnp.concatenate([r, i], axis=1), jnp.concatenate([i, -r], axis=1)], axis=0
                )
                for r, i in zip(turned_re, turned_im)
            )
            work = dot3(second, turned, NT)
            for j in range(ROWS_HERE):
                row = block * ROWS_HERE + j
                offset = gain[k, row] * work[16 * j : 16 * j + 16] - carry[k, row] * offset
                solved[pl.ds(16 * row, 16), :] = offset
        value = offset
        for row in range(ROWS - 2, -1, -1):
            value = solved[pl.ds(16 * row, 16), :] - pivot[k, row] * value
            solved[pl.ds(16 * row, 16), :] = value

        weight = 1.0 / (X * Z)
        kx = jnp.full((1, 128), first_mode + 256 * k, jnp.int32)
        weight = jnp.where(kx == 0, weight, 2.0 * weight)
        cos, sin = number(5) * weight, number(6) * weight
        sign = jnp.where(lanes[:1] < 64, -1.0, 1.0)
        for block in range(WALL):
            rows = pl.ds(512 * k + 128 * block, 128)
            value = halves_of(solved[pl.ds(128 * block, 128), :])
            mixed = dot3(wave_cos, value, NN) + sign * pltpu.roll(dot3(wave_sin, value, NN), 64, 1)
            turned = halves_of(mixed * cos + pltpu.roll(mixed, 64, 1) * sin)
            send_b[rows, :] = dot3(table(1), turned, NT)
        start(1, k, send_b, recv_b)

    sums = [0.0, 0.0]
    for k in range(2):
        arrive(1, k, send_b, recv_b)
        for parity in range(2):
            rows = pl.ds(512 * k + 256 * parity, 256)
            sums[parity] += dot3(halves_of(recv_b[rows, :].T), stream_rows(k, parity), NN)
    out[:, : X // 2] = sums[0] + sums[1]
    out[:, X // 2 :] = sums[0] - sums[1]
    for k in range(2):
        sent(0, k, send_a, recv_a)
        sent(1, k, send_b, recv_b)


def shards(source, spacing):
    plane = pltpu.VMEM((1024, 128), jnp.float32)
    coefficient = pltpu.VMEM((2, ROWS, 16, 128), jnp.float32)
    semaphores = pltpu.SemaphoreType.DMA((4,))
    pressure = pl.pallas_call(
        kernel,
        out_shape=pltpu.VMEM((ROWS_HERE * SPAN_HERE, X), jnp.float32),
        in_specs=[pl.BlockSpec(memory_space=pl.ANY)] * 3,
        out_specs=pl.BlockSpec(memory_space=pltpu.VMEM),
        scratch_shapes=[
            pltpu.SMEM((ROWS,), jnp.float32),
            pltpu.VMEM((ROWS_HERE * SPAN_HERE, X), jnp.float32),
            pltpu.VMEM((2560, 512), jnp.bfloat16),
            plane, plane, plane, plane, coefficient, coefficient, coefficient,
            pltpu.VMEM((512, 128), jnp.float32),
            semaphores, semaphores, semaphores, pltpu.SemaphoreType.DMA((7,)),
        ],
        compiler_params=pltpu.CompilerParams(
            collective_id=0, has_side_effects=True, vmem_limit_bytes=32 * 1024 * 1024
        ),
    )(
        pltpu.with_memory_space_constraint(spacing, pltpu.HBM),
        pltpu.with_memory_space_constraint(source.reshape(ROWS_HERE * SPAN_HERE, X), pltpu.HBM),
        pltpu.with_memory_space_constraint(jnp.asarray(tables()), pltpu.HBM),
    )
    return pressure.reshape(source.shape)


def solution(mesh):
    in_specs = (P("wall", "wide", None), P())
    out_specs = P("wall", "wide", None)
    return jax.shard_map(shards, mesh=mesh, in_specs=in_specs, out_specs=out_specs, check_vma=False)
```

```python
import functools
import math

import jax
import jax.numpy as jnp
import ml_dtypes
import numpy as np
from jax import lax
from jax.experimental import pallas as pl
from jax.experimental.pallas import tpu as pltpu
from jax.sharding import PartitionSpec as P

MESH = pl.DeviceIdType.MESH
TWO_PI = 2.0 * math.pi
X = 1024
Z = 1024
ROWS = 32
WALL = 4
WIDE = 64
SLOTS = WALL * WIDE
ROWS_HERE = ROWS // WALL
SPAN_HERE = Z // WIDE
PIECE = 2


def split_pair(table):
    high = table.astype(ml_dtypes.bfloat16)
    low = (table - high.astype(np.float64)).astype(ml_dtypes.bfloat16)
    return high, low


@functools.cache
def tables():
    x = np.arange(X // 2)
    slot = np.arange(SLOTS)
    mode = (2 * (slot % 128) + slot // 128)[None, :] + 256 * np.arange(2)[:, None]
    angle = TWO_PI * ((mode[..., None] * x) % X) / X
    stream = np.stack([np.cos(angle), -np.sin(angle)], axis=2).reshape(1024, 512)

    outer, inner = np.arange(64), np.arange(SPAN_HERE)
    angle = TWO_PI * ((outer[:, None] * outer[None, :]) % 64) / 64
    cos, sin = np.cos(angle), np.sin(angle)
    first = np.stack([np.stack([cos, sin], 2), np.stack([-sin, cos], 2)], 0)
    first = first.reshape(128, 128)
    angle = TWO_PI * ((inner[:, None] * inner[None, :]) % SPAN_HERE) / SPAN_HERE
    every_row = np.eye(ROWS_HERE)
    cos, sin = np.kron(every_row, np.cos(angle)), np.kron(every_row, np.sin(angle))
    angle = np.tile(TWO_PI * (outer[:, None] * inner[None, :]) / Z, (1, ROWS_HERE))
    turn_cos, turn_sin = np.cos(angle), np.sin(angle)
    twist = np.concatenate([turn_cos, turn_sin], axis=0)
    back_cos = np.concatenate([turn_cos.T, turn_cos.T], axis=1)
    back_sin = np.concatenate([-turn_sin.T, turn_sin.T], axis=1)
    small = np.concatenate(
        [first, first.T, cos, sin, twist, back_cos, back_sin], axis=1
    )
    small = np.pad(small, ((0, 0), (0, 128))).reshape(128, 2, 512).transpose(1, 0, 2).reshape(256, 512)
    return np.concatenate(split_pair(stream) + split_pair(small), axis=0)


def deltas(spanwise_first):
    steps = [
        (y, x, core, z)
        for y in range(4)
        for x in range(4)
        for core in range(2)
        for z in range(8)
        if (y, x, core, z) != (0, 0, 0, 0)
    ]
    across = lambda d: min(d[0], 4 - d[0]) + min(d[1], 4 - d[1])
    along = lambda d: min(d[3], 8 - d[3])
    if spanwise_first:
        return sorted(steps, key=lambda d: -along(d) - across(d))
    return sorted(steps, key=lambda d: (-across(d), -along(d)))


def halves_of(value):
    high = value.astype(jnp.bfloat16)
    return high, (value - high.astype(jnp.float32)).astype(jnp.bfloat16)


def dot3(left, right, contract):
    dot = functools.partial(
        lax.dot_general,
        dimension_numbers=(contract, ((), ())),
        preferred_element_type=jnp.float32,
    )
    return dot(left[0], right[0]) + (dot(left[0], right[1]) + dot(left[1], right[0]))


NN = ((1,), (0,))
NT = ((1,), (1,))


def kernel(
    spacing_far, source_far, packed_far, out,
    spacing, source, packed,
    send_a, recv_a, send_b, recv_b, gain, carry, pivot, solved,
    send_sem, recv_sem, own_sem, load_sem,
):
    wide, wall = lax.axis_index("wide"), lax.axis_index("wall")
    slot = wall * WIDE + wide
    core = lax.rem(wide, 2)
    x = lax.rem(lax.div(wide, 2), 4)
    y = lax.rem(lax.div(wide, 8), 4)
    z = lax.div(wide, 32) * 4 + wall
    at_core = [lax.rem(core + d, 2) for d in range(2)]
    at_x = [lax.rem(x + d, 4) * 2 for d in range(4)]
    at_y = [lax.rem(y + d, 4) * 8 for d in range(4)]
    z_all = [lax.rem(z + d, 8) for d in range(8)]
    at_high = [lax.div(v, 4) * 32 for v in z_all]
    at_wall = [lax.rem(v, 4) for v in z_all]

    def target(d):
        return at_y[d[0]] + at_x[d[1]] + at_core[d[2]] + at_high[d[3]], at_wall[d[3]]

    loads = [
        pltpu.make_async_copy(there, here, load_sem.at[index])
        for index, (there, here) in enumerate(
            [
                (source_far, source),
                (packed_far.at[pl.ds(0, 512)], packed.at[pl.ds(0, 512)]),
                (packed_far.at[pl.ds(1024, 512)], packed.at[pl.ds(1024, 512)]),
                (packed_far.at[pl.ds(512, 512)], packed.at[pl.ds(512, 512)]),
                (packed_far.at[pl.ds(1536, 512)], packed.at[pl.ds(1536, 512)]),
                (packed_far.at[pl.ds(2048, 512)], packed.at[pl.ds(2048, 512)]),
                (spacing_far, spacing),
            ]
        )
    ]
    barrier = pltpu.get_barrier_semaphore()
    for position, d in enumerate(deltas(True)):
        if position == 32:
            for load in loads:
                load.start()
        to_wide, to_wall = target(d)
        pl.semaphore_signal(
            barrier, inc=1, device_id={"wide": to_wide, "wall": to_wall}, device_id_type=MESH
        )
    order = deltas(False)

    def start(index, k, send, recv):
        index = 2 * index + k
        mine = pl.ds(pl.multiple_of(k * 512 + slot * PIECE, PIECE), PIECE)
        pltpu.make_async_copy(send.at[mine], recv.at[mine], own_sem.at[index]).start()
        for d in order:
            to_wide, to_wall = target(d)
            there = pl.multiple_of(k * 512 + (to_wall * WIDE + to_wide) * PIECE, PIECE)
            pltpu.make_async_remote_copy(
                src_ref=send.at[pl.ds(there, PIECE)],
                dst_ref=recv.at[mine],
                send_sem=send_sem.at[index],
                recv_sem=recv_sem.at[index],
                device_id={"wide": to_wide, "wall": to_wall},
                device_id_type=MESH,
            ).start()

    def arrive(index, k, send, recv):
        index = 2 * index + k
        mine = pl.ds(pl.multiple_of(k * 512 + slot * PIECE, PIECE), PIECE)
        pltpu.make_async_copy(send.at[mine], recv.at[mine], own_sem.at[index]).wait()
        rest = pl.ds(k * 512, (SLOTS - 1) * PIECE)
        pltpu.make_async_copy(send.at[rest], recv.at[rest], recv_sem.at[index]).wait()

    def sent(index, k, send, recv):
        rest = pl.ds(k * 512, (SLOTS - 1) * PIECE)
        pltpu.make_async_copy(send.at[rest], recv.at[rest], send_sem.at[2 * index + k]).wait()

    for load in loads[:3]:
        load.wait()
    left, right = source[:, : X // 2], source[:, X // 2 :]
    parts = halves_of(left + right), halves_of(left - right)

    def stream_rows(k, parity):
        base = 512 * k + 256 * parity
        return packed[pl.ds(base, 256), :], packed[pl.ds(1024 + base, 256), :]

    def transform(k):
        for parity in range(2):
            rows = pl.ds(512 * k + 256 * parity, 256)
            send_a[rows, :] = dot3(stream_rows(k, parity), parts[parity], NT)

    transform(0)
    pl.semaphore_wait(barrier, SLOTS - 1)
    start(0, 0, send_a, recv_a)
    for load in loads[3:]:
        load.wait()
    transform(1)
    start(0, 1, send_a, recv_a)

    lanes = lax.broadcasted_iota(jnp.int32, (16, 128), 1)
    digit = lax.broadcasted_iota(jnp.int32, (16, 128), 0)
    kz = 64 * digit + jnp.where(lanes >= 64, lanes - 64, lanes)
    kz = jnp.where(kz < Z // 2, kz, kz - Z)
    span_wave = kz.astype(jnp.float32) * (TWO_PI / Z)
    widths = [jnp.full((16, 128), spacing[j], jnp.float32) for j in range(ROWS)]
    edges = (
        [2.0 / widths[0]]
        + [2.0 / (widths[j] + widths[j + 1]) for j in range(ROWS - 1)]
        + [2.0 / widths[ROWS - 1]]
    )
    first_mode = 2 * lax.rem(slot, 128) + lax.div(slot, 128)
    wave_square, previous = [], []
    for k in range(2):
        kx = jnp.full((16, 128), first_mode + 256 * k, jnp.int32)
        stream_wave = kx.astype(jnp.float32) * (TWO_PI / X)
        wave_square.append(span_wave * span_wave + stream_wave * stream_wave)
        previous.append(jnp.zeros((16, 128), jnp.float32))
    for j in range(ROWS):
        lower, upper = edges[j], edges[j + 1]
        for k in range(2):
            divisor = -(lower + upper) - wave_square[k] * widths[j] - lower * previous[k]
            inverse = 1.0 / divisor
            previous[k] = upper * inverse
            pivot[k, j] = previous[k]
            gain[k, j] = widths[j] * inverse
            carry[k, j] = lower * inverse

    def table(index):
        high, columns = 2048 + 128 * (index // 4), pl.ds(128 * (index % 4), 128)
        return packed[pl.ds(high, 128), columns], packed[pl.ds(high + 256, 128), columns]

    def number(index):
        high, low = table(index)
        return high.astype(jnp.float32) + low.astype(jnp.float32)

    for k in range(2):
        arrive(0, k, send_a, recv_a)
        twist = number(4)
        cos, sin = twist[:64], twist[64:]
        wave_cos, wave_sin = table(2), table(3)
        second = tuple(jnp.concatenate([c, s], axis=1) for c, s in zip(wave_cos, wave_sin))
        offset = jnp.zeros((16, 128), jnp.float32)
        for block in range(WALL):
            rows = pl.ds(512 * k + 128 * block, 128)
            mixed = dot3(table(0), halves_of(recv_a[rows, :]), NN)
            re, im = mixed[:64], mixed[64:]
            turned_re = halves_of(re * cos + im * sin)
            turned_im = halves_of(im * cos - re * sin)
            turned = tuple(
                jnp.concatenate(
                    [jnp.concatenate([r, i], axis=1), jnp.concatenate([i, -r], axis=1)], axis=0
                )
                for r, i in zip(turned_re, turned_im)
            )
            work = dot3(second, turned, NT)
            for j in range(ROWS_HERE):
                row = block * ROWS_HERE + j
                offset = gain[k, row] * work[16 * j : 16 * j + 16] - carry[k, row] * offset
                solved[pl.ds(16 * row, 16), :] = offset
        value = offset
        for row in range(ROWS - 2, -1, -1):
            value = solved[pl.ds(16 * row, 16), :] - pivot[k, row] * value
            solved[pl.ds(16 * row, 16), :] = value

        weight = 1.0 / (X * Z)
        kx = jnp.full((1, 128), first_mode + 256 * k, jnp.int32)
        weight = jnp.where(kx == 0, weight, 2.0 * weight)
        cos, sin = number(5) * weight, number(6) * weight
        sign = jnp.where(lanes[:1] < 64, -1.0, 1.0)
        for block in range(WALL):
            rows = pl.ds(512 * k + 128 * block, 128)
            value = halves_of(solved[pl.ds(128 * block, 128), :])
            mixed = dot3(wave_cos, value, NN) + sign * pltpu.roll(dot3(wave_sin, value, NN), 64, 1)
            turned = halves_of(mixed * cos + pltpu.roll(mixed, 64, 1) * sin)
            send_b[rows, :] = dot3(table(1), turned, NT)
        start(1, k, send_b, recv_b)

    sums = [0.0, 0.0]
    for k in range(2):
        arrive(1, k, send_b, recv_b)
        for parity in range(2):
            rows = pl.ds(512 * k + 256 * parity, 256)
            sums[parity] += dot3(halves_of(recv_b[rows, :].T), stream_rows(k, parity), NN)
    out[:, : X // 2] = sums[0] + sums[1]
    out[:, X // 2 :] = sums[0] - sums[1]
    for k in range(2):
        sent(0, k, send_a, recv_a)
        sent(1, k, send_b, recv_b)


def shards(source, spacing):
    plane = pltpu.VMEM((1024, 128), jnp.float32)
    coefficient = pltpu.VMEM((2, ROWS, 16, 128), jnp.float32)
    semaphores = pltpu.SemaphoreType.DMA((4,))
    pressure = pl.pallas_call(
        kernel,
        out_shape=pltpu.VMEM((ROWS_HERE * SPAN_HERE, X), jnp.float32),
        in_specs=[pl.BlockSpec(memory_space=pl.ANY)] * 3,
        out_specs=pl.BlockSpec(memory_space=pltpu.VMEM),
        scratch_shapes=[
            pltpu.SMEM((ROWS,), jnp.float32),
            pltpu.VMEM((ROWS_HERE * SPAN_HERE, X), jnp.float32),
            pltpu.VMEM((2560, 512), jnp.bfloat16),
            plane, plane, plane, plane, coefficient, coefficient, coefficient,
            pltpu.VMEM((512, 128), jnp.float32),
            semaphores, semaphores, semaphores, pltpu.SemaphoreType.DMA((7,)),
        ],
        compiler_params=pltpu.CompilerParams(
            collective_id=0, has_side_effects=True, vmem_limit_bytes=32 * 1024 * 1024
        ),
    )(
        pltpu.with_memory_space_constraint(spacing, pltpu.HBM),
        pltpu.with_memory_space_constraint(source.reshape(ROWS_HERE * SPAN_HERE, X), pltpu.HBM),
        pltpu.with_memory_space_constraint(jnp.asarray(tables()), pltpu.HBM),
    )
    return pressure.reshape(source.shape)


def solution(mesh):
    in_specs = (P("wall", "wide", None), P())
    out_specs = P("wall", "wide", None)
    return jax.shard_map(shards, mesh=mesh, in_specs=in_specs, out_specs=out_specs, check_vma=False)
```
